32 devices in a mesh: tm: 2 (over x), space: 16 (over z, y, core).
Axes of the slice: x: 2, y: 2, z: 4, core: 2. Of those that a mesh axis runs over, the one named last changes fastest.
Arguments:
- states: float32 [4, 128, 64, 128], P('tm', 'space'), may hold values from -1.2 to 1.2
- kappa: float32 [128, 64, 128], P('space'), may hold values from 0.02 to 0.15
- rate: float32 [128, 64, 128], P('space'), may hold values from 0.02 to 0.2
Outputs:
- ends: float32 [4, 128, 64, 128], P('tm', 'space')
The draws below stay inside these ranges and needn't reach their ends.
All inputs are finite; a program needn't handle non-finite values.
Results may differ from the reference program's by a relative error of at most 0.00013.
Values sent between devices are 32-bit elements; how exact they have to be, the bound alone decides.
A program may use at most 64 MiB of HBM per device.

```python
import math
import jax
import jax.numpy as jnp

NY = 64
NZ = 128
STEPS = 12
COARSE = 3
WINDOWS = 4
NX = 128


def level_of(key, dims, split, least, largest):
    def one(dim, parts):
        heights = jax.random.uniform(jax.random.fold_in(jax.random.fold_in(key, 6), dim), (parts,), jnp.float32, least / len(split), largest / len(split))
        return jnp.repeat(jnp.exp(heights), dims[dim] // parts).reshape((-1,) + (1,) * (len(dims) - dim - 1))

    gain = one(*split[0])
    for cut in split[1:]:
        gain = gain * one(*cut)
    return gain


def setup_inputs(seed: int = 0) -> dict:
    arg_keys = jax.random.split(jax.random.key(seed), 4)
    return {
        "states": jnp.clip(jax.random.uniform(arg_keys[0], (WINDOWS, NX, NY, NZ), jnp.float32, -1.2, 1.2) * level_of(arg_keys[0], (WINDOWS, NX, NY, NZ), ((0, 2), (1, 16)), -0.4, 0.0), -1.2, 1.2),
        "kappa": jnp.clip(jnp.exp(math.log(0.15) - 2.014903 * jax.random.uniform(arg_keys[1], (NX, NY, NZ), jnp.float32) ** level_of(arg_keys[1], (NX, NY, NZ), ((0, 16),), -0.2, 0.2)), 0.02, 0.15),
        "rate": jnp.clip(jnp.exp(math.log(0.2) - 2.3025851 * jax.random.uniform(arg_keys[2], (NX, NY, NZ), jnp.float32) ** level_of(arg_keys[2], (NX, NY, NZ), ((0, 16),), -0.2, 0.2)), 0.02, 0.2),
    }


def shifted(array, offset):
    lead = array.ndim - 3
    sizes = array.shape[-3:]
    picks = tuple(slice(1 + offset[axis_no], sizes[axis_no] - 1 + offset[axis_no]) for axis_no in range(3))
    return array[(slice(None),) * lead + picks]


def grid_step(field_ext, kappa_ext, rate_mid):
    padded = jnp.pad(field_ext, ((0, 0), (0, 0), (1, 1), (1, 1)))
    kappa_pad = jnp.pad(kappa_ext, ((0, 0), (1, 1), (1, 1)))
    centre = padded[:, 1:-1, 1:-1, 1:-1]
    kappa_mid = kappa_pad[1:-1, 1:-1, 1:-1]
    change = jnp.zeros_like(centre)
    for offset in ((1, 0, 0), (-1, 0, 0), (0, 1, 0), (0, -1, 0), (0, 0, 1), (0, 0, -1)):
        change = change + 0.5 * (kappa_mid + shifted(kappa_pad, offset)) * (shifted(padded, offset) - centre)
    return centre + change + rate_mid * (centre - centre * centre * centre)


def restrict(field_now):
    lead = field_now.shape[:-3]
    sizes = field_now.shape[-3:]
    blocks = field_now.reshape(lead + (sizes[0] // 2, 2, sizes[1] // 2, 2, sizes[2] // 2, 2))
    return jnp.mean(blocks, axis=(-5, -3, -1))


def prolong(coarse_field):
    return jnp.repeat(jnp.repeat(jnp.repeat(coarse_field, 2, axis=-3), 2, axis=-2), 2, axis=-1)


def pad_rows(field_now):
    return jnp.pad(field_now, ((0, 0), (1, 1), (0, 0), (0, 0)))


def reference(states, kappa, rate):
    kappa_ext = jnp.pad(kappa, ((1, 1), (0, 0), (0, 0)))
    fine_end = []
    for window in range(WINDOWS):
        field_now = states[window][None]
        for counter in range(STEPS):
            field_now = grid_step(pad_rows(field_now), kappa_ext, rate)
        fine_end.append(field_now[0])
    coarse_kappa = jnp.pad(restrict(kappa), ((1, 1), (0, 0), (0, 0)))
    coarse_rate = 4.0 * restrict(rate)

    def coarse_prop(coarse_field):
        for sweeps in range(COARSE):
            coarse_field = grid_step(pad_rows(coarse_field), coarse_kappa, coarse_rate)
        return coarse_field

    old_coarse = coarse_prop(restrict(states))
    carried = restrict(states[0:1])
    results = []
    for window in range(WINDOWS):
        moved = coarse_prop(carried)
        results.append(fine_end[window] + prolong(moved[0] - old_coarse[window]))
        carried = (restrict(fine_end[window]) - old_coarse[window])[None] + moved
    return jnp.stack(results)
```

```python
import functools

import jax
import jax.numpy as jnp
from jax import lax
from jax.experimental import pallas as pl
from jax.experimental.pallas import tpu as pltpu
from jax.sharding import PartitionSpec as P

STEPS = 12
COARSE = 3
DEPTH = 2
ROUNDS = STEPS // DEPTH
MESH = pl.DeviceIdType.MESH
A, R, XP, XM, YP, YM, ZP, ZM = range(8)


def y_next(plane):
    rows = plane.shape[0]
    return jnp.concatenate([plane[8:rows], pltpu.roll(plane[0:8], 7, 0)], axis=0)


def y_prev(plane):
    rows = plane.shape[0]
    return jnp.concatenate([pltpu.roll(plane[rows - 8 : rows], 1, 0), plane[0 : rows - 8]], axis=0)


def z_next(plane, stride):
    return pltpu.roll(plane, plane.shape[1] - stride, 1)


def z_prev(plane, stride):
    return pltpu.roll(plane, stride, 1)


def edge_masks(rows, lanes, stride):
    row = lax.broadcasted_iota(jnp.int32, (rows, lanes), 0)
    lane = lax.broadcasted_iota(jnp.int32, (rows, lanes), 1)
    return (
        jnp.where(row == rows - 1, 0.0, 1.0),
        jnp.where(row == 0, 0.0, 1.0),
        jnp.where(lane >= lanes - stride, 0.0, 1.0),
        jnp.where(lane < stride, 0.0, 1.0),
    )


def make_coefs(coef, field, reaction, low, high, stride, row_valid):
    rows, lanes = field.shape[-2:]
    y_up, y_down, z_up, z_down = edge_masks(rows, lanes, stride)

    def body(i, _):
        k = field[i]
        r = reaction[i]
        valid = row_valid(i)
        xp = 0.5 * (k + field[i + 1])
        xm = 0.5 * (k + field[i - 1])
        yp = 0.5 * (k + y_next(k) * y_up)
        ym = 0.5 * (k + y_prev(k) * y_down)
        zp = 0.5 * (k + z_next(k, stride) * z_up)
        zm = 0.5 * (k + z_prev(k, stride) * z_down)
        coef[A, i] = (1.0 + r - ((xp + xm) + (yp + ym) + (zp + zm))) * valid
        coef[R, i] = r * valid
        coef[XP, i] = xp * valid
        coef[XM, i] = xm * valid
        coef[YP, i] = yp * y_up * valid
        coef[YM, i] = ym * y_down * valid
        coef[ZP, i] = zp * z_up * valid
        coef[ZM, i] = zm * z_down * valid
        return 0

    lax.fori_loop(low, high, body, 0)


def grid_step(source, target, coef, low, high, stride):
    def body(i, _):
        u = source[i]
        total = u * (coef[A, i] - coef[R, i] * (u * u))
        total = total + (coef[XP, i] * source[i + 1] + coef[XM, i] * source[i - 1])
        total = total + (coef[YP, i] * y_next(u) + coef[YM, i] * y_prev(u))
        total = total + (coef[ZP, i] * z_next(u, stride) + coef[ZM, i] * z_prev(u, stride))
        target[i] = total
        return 0

    lax.fori_loop(low, high, body, 0)


def restrict_rows(first, second):
    both = first + second
    rows, lanes = both.shape
    pairs = jnp.concatenate(
        [both[j : j + 8] + both[j + 8 : j + 16] for j in range(0, rows, 16)], axis=0
    )
    lane = lax.broadcasted_iota(jnp.int32, pairs.shape, 1)
    other = jnp.where(lane % 2 == 0, z_next(pairs, 1), z_prev(pairs, 1))
    return (pairs + other) * 0.125


def prolong_rows(plane):
    rows = plane.shape[0]
    return jnp.concatenate(
        [plane[j : j + 8] for j in range(0, rows, 8) for _ in range(2)], axis=0
    )


def kernel(
    count, groups, states, kappa, rate, out,
    u, temp, raw_u, raw_k, raw_r, kx, rx, coef,
    kc, rc, ccoef, ctemp, cstate, old, chain, newer, passed, outgoing,
    send, recv, tm_send, tm_recv,
):
    windows, n, rows, lanes = states.shape
    ext = n + 2 * DEPTH
    nc = n // 2
    side = COARSE
    cext = nc + 2 * side
    per = rows // 8
    rate_rows = max(DEPTH - 1, 1)
    me = lax.axis_index("space")
    group = lax.axis_index("tm")
    left = lax.rem(me + count - 1, count)
    right = lax.rem(me + 1, count)
    has_left = me > 0
    has_right = me < count - 1

    def when_left(fn):
        pl.when(has_left)(fn)

    def when_right(fn):
        pl.when(has_right)(fn)

    class Swap:
        def __init__(self, head, tail, left_halo, right_halo, slot):
            self.to_left = pltpu.make_async_remote_copy(
                src_ref=head, dst_ref=right_halo, send_sem=send.at[slot, 0],
                recv_sem=recv.at[slot, 1], device_id={"space": left}, device_id_type=MESH,
            )
            self.to_right = pltpu.make_async_remote_copy(
                src_ref=tail, dst_ref=left_halo, send_sem=send.at[slot, 1],
                recv_sem=recv.at[slot, 0], device_id={"space": right}, device_id_type=MESH,
            )

        def start(self):
            when_left(self.to_left.start)
            when_right(self.to_right.start)

        def arrived(self):
            when_left(self.to_right.wait_recv)
            when_right(self.to_left.wait_recv)

        def sent(self):
            when_left(self.to_left.wait_send)
            when_right(self.to_right.wait_send)

    def padded_swap(ref, width, depth, slot):
        return Swap(
            ref.at[pl.ds(depth, depth)], ref.at[pl.ds(width, depth)],
            ref.at[pl.ds(0, depth)], ref.at[pl.ds(width + depth, depth)], slot,
        )

    slot_k, slot_r, slot_kc, slot_rc = (windows + i for i in range(4))
    slot_old = windows + 4
    slot_chain = 2 * windows + 4
    slot_round = 3 * windows + 4

    def raw_swap(source, target, depth, slot):
        return Swap(
            source.at[pl.ds(0, depth)], source.at[pl.ds(n - depth, depth)],
            target.at[0], target.at[1], slot,
        )

    first_u = [raw_swap(states.at[w], raw_u.at[w], DEPTH, w) for w in range(windows)]
    first_k = raw_swap(kappa, raw_k, DEPTH, slot_k)
    first_r = raw_swap(rate, raw_r, rate_rows, slot_r)
    coarse_k = padded_swap(kc, nc, side, slot_kc)
    coarse_r = padded_swap(rc, nc, side, slot_rc)
    coarse_old = [padded_swap(cstate.at[w], nc, side, slot_old + w) for w in range(windows)]
    coarse_chain = [padded_swap(chain.at[w], nc, side, slot_chain + w) for w in range(windows)]

    def round_swap(r, w):
        return padded_swap(u.at[r, w], n, DEPTH, slot_round + r * windows + w)

    barrier = pltpu.get_barrier_semaphore()

    def greet(where):
        pl.semaphore_signal(barrier, inc=1, device_id=where, device_id_type=MESH)

    when_left(lambda: greet({"space": left}))
    when_right(lambda: greet({"space": right}))
    pl.when(group > 0)(lambda: greet({"tm": lax.rem(group + groups - 1, groups)}))
    pl.when(group < groups - 1)(lambda: greet({"tm": lax.rem(group + 1, groups)}))

    def load_plane(ref, *index):
        return jnp.concatenate(
            [ref[(*index, pl.ds(j, 8, stride=per), slice(None))] for j in range(per)], axis=0
        )

    def fill_own(i, _):
        kx[DEPTH + i] = load_plane(kappa, i)
        rx[DEPTH + i] = load_plane(rate, i)
        for w in range(windows):
            u[0, w, DEPTH + i] = load_plane(states, w, i)
        return 0

    lax.fori_loop(0, n, fill_own, 0)

    def zero(ref, low, size):
        ref[pl.ds(low, size)] = jnp.zeros((size,) + ref.shape[1:], jnp.float32)

    def zero_side(fine_low, coarse_low):
        zero(kx, fine_low, DEPTH)
        zero(rx, fine_low, DEPTH)
        zero(kc, coarse_low, side)
        zero(rc, coarse_low, side)
        for w in range(windows):
            zero(cstate.at[w], coarse_low, side)
            zero(chain.at[w], coarse_low, side)
            for r in range(ROUNDS):
                zero(u.at[r, w], fine_low, DEPTH)

    pl.when(me == 0)(lambda: zero_side(0, 0))
    pl.when(me == count - 1)(lambda: zero_side(n + DEPTH, nc + side))

    peers = [has_left, has_right, group > 0, group < groups - 1]
    pl.semaphore_wait(barrier, sum(jnp.where(there, 1, 0) for there in peers))

    first_k.start()
    first_r.start()
    for swap in first_u:
        swap.start()

    def coarse_rows(i, _):
        base = DEPTH + 2 * i
        kc[side + i] = restrict_rows(kx[base], kx[base + 1])
        rc[side + i] = 4.0 * restrict_rows(rx[base], rx[base + 1])
        for w in range(windows):
            cstate[w, side + i] = restrict_rows(u[0, w, base], u[0, w, base + 1])
        return 0

    lax.fori_loop(0, nc, coarse_rows, 0)
    coarse_k.start()
    coarse_r.start()
    for swap in coarse_old:
        swap.start()

    def fine_valid(i):
        place = me * n + i - DEPTH
        return jnp.where((place >= 0) & (place < count * n), 1.0, 0.0)

    def coarse_valid(i):
        place = me * nc + i - side
        return jnp.where((place >= 0) & (place < count * nc), 1.0, 0.0)

    make_coefs(coef, kx, rx, DEPTH + 1, DEPTH + n - 1, 1, fine_valid)

    first_k.arrived()
    first_r.arrived()

    def unpack_k(which, low, rate_low):
        for i in range(DEPTH):
            kx[low + i] = load_plane(raw_k, which, i)
        for i in range(rate_rows):
            rx[rate_low + i] = load_plane(raw_r, which, i)

    when_left(lambda: unpack_k(0, 0, DEPTH - rate_rows))
    when_right(lambda: unpack_k(1, n + DEPTH, n + DEPTH))
    make_coefs(coef, kx, rx, 1, DEPTH + 1, 1, fine_valid)
    make_coefs(coef, kx, rx, DEPTH + n - 1, ext - 1, 1, fine_valid)

    def fine_round(r, w):
        source = u.at[r, w]
        for k in range(1, DEPTH + 1):
            target = u.at[r + 1, w] if k == DEPTH else temp.at[k % 2]
            grid_step(source, target, coef, k, ext - k, 1)
            source = target

    def unpack_u(w, which, low):
        for i in range(DEPTH):
            u[0, w, low + i] = load_plane(raw_u, w, which, i)

    for w in range(windows):
        first_u[w].arrived()
        when_left(functools.partial(unpack_u, w, 0, 0))
        when_right(functools.partial(unpack_u, w, 1, n + DEPTH))
        fine_round(0, w)
        if ROUNDS > 1:
            round_swap(1, w).start()

    def coarse_run(source, target):
        for k in range(1, COARSE):
            dest = ctemp.at[k % 2]
            grid_step(source, dest, ccoef, k, cext - k, 2)
            source = dest
        grid_step(source, target, ccoef, COARSE, cext - COARSE, 2)

    coarse_k.arrived()
    coarse_r.arrived()
    make_coefs(ccoef, kc, rc, 1, cext - 1, 2, coarse_valid)
    for w in range(windows):
        coarse_old[w].arrived()
        coarse_run(cstate.at[w], old.at[w])

    def middle(r, _):
        for w in range(windows):
            round_swap(r, w).arrived()
            fine_round(r, w)
            round_swap(r + 1, w).start()
        return 0

    lax.fori_loop(1, ROUNDS - 1, middle, 0)

    def deltas(w, i):
        base = DEPTH + 2 * i
        ends = restrict_rows(u[ROUNDS, w, base], u[ROUNDS, w, base + 1])
        return (ends - old[w, side + i]) + newer[w, side + i]

    def carry_on(w):
        def body(i, _):
            chain[w + 1, side + i] = deltas(w, i)
            return 0

        lax.fori_loop(0, nc, body, 0)

    def take_old():
        newer[0, pl.ds(side, nc)] = old[0, pl.ds(side, nc)]

    incoming = pltpu.make_async_remote_copy(
        src_ref=outgoing, dst_ref=passed, send_sem=tm_send, recv_sem=tm_recv,
        device_id={"tm": lax.rem(group + 1, groups)}, device_id_type=MESH,
    ) if groups > 1 else None

    for w in range(windows):
        if ROUNDS > 1:
            round_swap(ROUNDS - 1, w).arrived()
            fine_round(ROUNDS - 1, w)
        if w == 0:
            pl.when(group == 0)(take_old)
            if windows > 1:
                def start_chain():
                    carry_on(0)
                    coarse_chain[1].start()

                pl.when(group == 0)(start_chain)

    if groups > 1:
        def from_before():
            incoming.wait_recv()
            chain[0, pl.ds(side, nc)] = passed[...]
            coarse_chain[0].start()
            coarse_chain[0].arrived()
            coarse_run(chain.at[0], newer.at[0])
            if windows > 1:
                carry_on(0)
                coarse_chain[1].start()

        pl.when(group > 0)(from_before)

    for w in range(1, windows):
        coarse_chain[w].arrived()
        coarse_run(chain.at[w], newer.at[w])
        if w + 1 < windows:
            carry_on(w)
            coarse_chain[w + 1].start()

    if groups > 1:
        def to_next():
            def body(i, _):
                outgoing[i] = deltas(windows - 1, i)
                return 0

            lax.fori_loop(0, nc, body, 0)
            incoming.start()

        pl.when(group < groups - 1)(to_next)

    def finish(i, _):
        for w in range(windows):
            change = prolong_rows(newer[w, side + i] - old[w, side + i])
            for half in range(2):
                plane = u[ROUNDS, w, DEPTH + 2 * i + half] + change
                for j in range(per):
                    out[w, 2 * i + half, pl.ds(j, 8, stride=per), :] = plane[8 * j : 8 * j + 8]
        return 0

    lax.fori_loop(0, nc, finish, 0)

    for swap in [first_k, first_r, coarse_k, coarse_r] + first_u + coarse_old + coarse_chain[1:]:
        swap.sent()

    def rounds_sent(r, _):
        for w in range(windows):
            round_swap(r, w).sent()
        return 0

    lax.fori_loop(1, ROUNDS, rounds_sent, 0)
    if groups > 1:
        pl.when(group > 0)(coarse_chain[0].sent)
        pl.when(group < groups - 1)(incoming.wait_send)


def shards(count, groups, states, kappa, rate):
    windows, n, rows, lanes = states.shape
    ext = n + 2 * DEPTH
    nc = n // 2
    cext = nc + 2 * COARSE
    crows = rows // 2
    slots = 3 * windows + 4 + ROUNDS * windows
    f32 = jnp.float32
    vmem = pl.BlockSpec(memory_space=pltpu.VMEM)
    return pl.pallas_call(
        functools.partial(kernel, count, groups),
        out_shape=jax.ShapeDtypeStruct(states.shape, f32),
        in_specs=[vmem] * 3,
        out_specs=vmem,
        scratch_shapes=[
            pltpu.VMEM((ROUNDS + 1, windows, ext, rows, lanes), f32),
            pltpu.VMEM((2, ext, rows, lanes), f32),
            pltpu.VMEM((windows, 2, DEPTH, rows, lanes), f32),
            pltpu.VMEM((2, DEPTH, rows, lanes), f32),
            pltpu.VMEM((2, max(DEPTH - 1, 1), rows, lanes), f32),
            pltpu.VMEM((ext, rows, lanes), f32),
            pltpu.VMEM((ext, rows, lanes), f32),
            pltpu.VMEM((8, ext, rows, lanes), f32),
            pltpu.VMEM((cext, crows, lanes), f32),
            pltpu.VMEM((cext, crows, lanes), f32),
            pltpu.VMEM((8, cext, crows, lanes), f32),
            pltpu.VMEM((2, cext, crows, lanes), f32),
            pltpu.VMEM((windows, cext, crows, lanes), f32),
            pltpu.VMEM((windows, cext, crows, lanes), f32),
            pltpu.VMEM((windows, cext, crows, lanes), f32),
            pltpu.VMEM((windows, cext, crows, lanes), f32),
            pltpu.VMEM((nc, crows, lanes), f32),
            pltpu.VMEM((nc, crows, lanes), f32),
            pltpu.SemaphoreType.DMA((slots, 2)),
            pltpu.SemaphoreType.DMA((slots, 2)),
            pltpu.SemaphoreType.DMA,
            pltpu.SemaphoreType.DMA,
        ],
        compiler_params=pltpu.CompilerParams(
            collective_id=0, has_side_effects=True, vmem_limit_bytes=40 * 1024 * 1024
        ),
    )(states, kappa, rate)


def solution(mesh):
    in_specs = (P("tm", "space", None, None), P("space", None, None), P("space", None, None))
    out_specs = P("tm", "space", None, None)
    body = functools.partial(shards, mesh.shape["space"], mesh.shape["tm"])
    return jax.shard_map(body, mesh=mesh, in_specs=in_specs, out_specs=out_specs, check_vma=False)
```

```python
import functools

import jax
import jax.numpy as jnp
from jax import lax
from jax.experimental import pallas as pl
from jax.experimental.pallas import tpu as pltpu
from jax.sharding import PartitionSpec as P

STEPS = 12
COARSE = 3
DEPTH = 2
ROUNDS = STEPS // DEPTH
MESH = pl.DeviceIdType.MESH
A, R, XP, YP, ZP = range(5)


def y_next(plane):
    rows = plane.shape[0]
    return jnp.concatenate([plane[8:rows], pltpu.roll(plane[0:8], 7, 0)], axis=0)


def y_prev(plane):
    rows = plane.shape[0]
    return jnp.concatenate([pltpu.roll(plane[rows - 8 : rows], 1, 0), plane[0 : rows - 8]], axis=0)


def z_next(plane, stride):
    return pltpu.roll(plane, plane.shape[1] - stride, 1)


def z_prev(plane, stride):
    return pltpu.roll(plane, stride, 1)


def edge_masks(rows, lanes, stride):
    row = lax.broadcasted_iota(jnp.int32, (rows, lanes), 0)
    lane = lax.broadcasted_iota(jnp.int32, (rows, lanes), 1)
    return (
        jnp.where(row == rows - 1, 0.0, 1.0),
        jnp.where(row == 0, 0.0, 1.0),
        jnp.where(lane >= lanes - stride, 0.0, 1.0),
        jnp.where(lane < stride, 0.0, 1.0),
    )


def make_coefs(coef, field, reaction, low, high, stride, row_valid):
    rows, lanes = field.shape[-2:]
    y_up, y_down, z_up, z_down = edge_masks(rows, lanes, stride)
    for i in range(low, high):
        k = field[i]
        r = reaction[i]
        valid = row_valid(i)
        xp = 0.5 * (k + field[i + 1])
        xm = 0.5 * (k + field[i - 1])
        yp = 0.5 * (k + y_next(k) * y_up)
        ym = 0.5 * (k + y_prev(k) * y_down)
        zp = 0.5 * (k + z_next(k, stride) * z_up)
        zm = 0.5 * (k + z_prev(k, stride) * z_down)
        coef[A, i] = (1.0 + r - ((xp + xm) + (yp + ym) + (zp + zm))) * valid
        coef[R, i] = r * valid
        coef[XP, i] = xp * (valid * row_valid(i + 1))
        coef[YP, i] = yp * (y_up * valid)
        coef[ZP, i] = zp * (z_up * valid)


def first_face(coef, field, low, row_valid):
    both = row_valid(low) * row_valid(low + 1)
    coef[XP, low] = (0.5 * both) * (field[low] + field[low + 1])


def grid_step(source, target, coef, low, high, stride):
    before, u, before_face = source[low - 1], source[low], coef[XP, low - 1]
    for i in range(low, high):
        after = source[i + 1]
        face = coef[XP, i]
        y_face = coef[YP, i]
        z_face = coef[ZP, i]
        total = u * (coef[A, i] - coef[R, i] * (u * u))
        total = total + (face * after + before_face * before)
        total = total + (y_face * y_next(u) + y_prev(y_face * u))
        total = total + (z_face * z_next(u, stride) + z_prev(z_face * u, stride))
        target[i] = total
        before, u, before_face = u, after, face


def restrict_rows(first, second):
    both = first + second
    rows, lanes = both.shape
    pairs = jnp.concatenate(
        [both[j : j + 8] + both[j + 8 : j + 16] for j in range(0, rows, 16)], axis=0
    )
    lane = lax.broadcasted_iota(jnp.int32, pairs.shape, 1)
    other = jnp.where(lane % 2 == 0, z_next(pairs, 1), z_prev(pairs, 1))
    return (pairs + other) * 0.125


def prolong_rows(plane):
    rows = plane.shape[0]
    return jnp.concatenate(
        [plane[j : j + 8] for j in range(0, rows, 8) for _ in range(2)], axis=0
    )


def kernel(
    count, groups, states, kappa, rate, out,
    own_u, own_k, own_r, u, temp, raw_u, raw_k, raw_r, kx, rx, coef,
    kc, rc, ccoef, ctemp, cstate, old, chain, newer, passed, outgoing,
    send, recv, tm_send, tm_recv, local,
):
    windows, n, rows, lanes = states.shape
    ext = n + 2 * DEPTH
    nc = n // 2
    side = COARSE
    cext = nc + 2 * side
    per = rows // 8
    rate_rows = max(DEPTH - 1, 1)
    me = lax.axis_index("space")
    group = lax.axis_index("tm")
    left = lax.rem(me + count - 1, count)
    right = lax.rem(me + 1, count)
    has_left = me > 0
    has_right = me < count - 1

    def when_left(fn):
        pl.when(has_left)(fn)

    def when_right(fn):
        pl.when(has_right)(fn)

    class Swap:
        def __init__(self, head, tail, left_halo, right_halo, slot):
            self.to_left = pltpu.make_async_remote_copy(
                src_ref=head, dst_ref=right_halo, send_sem=send.at[slot, 0],
                recv_sem=recv.at[slot, 1], device_id={"space": left}, device_id_type=MESH,
            )
            self.to_right = pltpu.make_async_remote_copy(
                src_ref=tail, dst_ref=left_halo, send_sem=send.at[slot, 1],
                recv_sem=recv.at[slot, 0], device_id={"space": right}, device_id_type=MESH,
            )

        def start(self):
            when_left(self.to_left.start)
            when_right(self.to_right.start)

        def arrived(self):
            when_left(self.to_right.wait_recv)
            when_right(self.to_left.wait_recv)

        def sent(self):
            when_left(self.to_left.wait_send)
            when_right(self.to_right.wait_send)

    def padded_swap(ref, width, depth, slot):
        return Swap(
            ref.at[pl.ds(depth, depth)], ref.at[pl.ds(width, depth)],
            ref.at[pl.ds(0, depth)], ref.at[pl.ds(width + depth, depth)], slot,
        )

    slot_k, slot_r, slot_kc, slot_rc = (windows + i for i in range(4))
    slot_old = windows + 4
    slot_chain = 2 * windows + 4
    slot_round = 3 * windows + 4

    def raw_swap(source, target, depth, slot):
        return Swap(
            source.at[pl.ds(0, depth)], source.at[pl.ds(n - depth, depth)],
            target.at[0], target.at[1], slot,
        )

    first_u = [raw_swap(states.at[w], raw_u.at[w], DEPTH, w) for w in range(windows)]
    first_k = raw_swap(kappa, raw_k, DEPTH, slot_k)
    first_r = raw_swap(rate, raw_r, rate_rows, slot_r)
    coarse_k = padded_swap(kc, nc, side, slot_kc)
    coarse_r = padded_swap(rc, nc, side, slot_rc)
    coarse_old = [padded_swap(cstate.at[w], nc, side, slot_old + w) for w in range(windows)]
    coarse_chain = [padded_swap(chain.at[w], nc, side, slot_chain + w) for w in range(windows)]

    def round_swap(r, w):
        return padded_swap(u.at[r, w], n, DEPTH, slot_round + r * windows + w)

    loads = [
        pltpu.make_async_copy(source, target, local.at[i])
        for i, (source, target) in enumerate(((kappa, own_k), (rate, own_r), (states, own_u)))
    ]
    for load in loads:
        load.start()
    barrier = pltpu.get_barrier_semaphore()

    def greet(where):
        pl.semaphore_signal(barrier, inc=1, device_id=where, device_id_type=MESH)

    when_left(lambda: greet({"space": left}))
    when_right(lambda: greet({"space": right}))
    pl.when(group > 0)(lambda: greet({"tm": lax.rem(group + groups - 1, groups)}))
    pl.when(group < groups - 1)(lambda: greet({"tm": lax.rem(group + 1, groups)}))

    def load_plane(ref, *index):
        return jnp.concatenate(
            [ref[(*index, pl.ds(j, 8, stride=per), slice(None))] for j in range(per)], axis=0
        )

    def zero(ref, low, size):
        ref[pl.ds(low, size)] = jnp.zeros((size,) + ref.shape[1:], jnp.float32)

    def zero_side(fine_low, coarse_low):
        zero(kx, fine_low, DEPTH)
        zero(rx, fine_low, DEPTH)
        zero(kc, coarse_low, side)
        zero(rc, coarse_low, side)
        for w in range(windows):
            zero(cstate.at[w], coarse_low, side)
            zero(chain.at[w], coarse_low, side)
            for r in range(ROUNDS):
                zero(u.at[r, w], fine_low, DEPTH)

    pl.when(me == 0)(lambda: zero_side(0, 0))
    pl.when(me == count - 1)(lambda: zero_side(n + DEPTH, nc + side))

    peers = [has_left, has_right, group > 0, group < groups - 1]
    pl.semaphore_wait(barrier, sum(jnp.where(there, 1, 0) for there in peers))

    first_k.start()
    first_r.start()
    for swap in first_u:
        swap.start()

    loads[0].wait()
    for i in range(n):
        kx[DEPTH + i] = load_plane(own_k, i)
    loads[1].wait()
    for i in range(n):
        rx[DEPTH + i] = load_plane(own_r, i)
    loads[2].wait()
    for w in range(windows):
        for i in range(n):
            u[0, w, DEPTH + i] = load_plane(own_u, w, i)

    def coarse_rows(i, _):
        base = DEPTH + 2 * i
        kc[side + i] = restrict_rows(kx[base], kx[base + 1])
        rc[side + i] = 4.0 * restrict_rows(rx[base], rx[base + 1])
        for w in range(windows):
            cstate[w, side + i] = restrict_rows(u[0, w, base], u[0, w, base + 1])
        return 0

    for i in range(nc):
        coarse_rows(i, 0)
    coarse_k.start()
    coarse_r.start()
    for swap in coarse_old:
        swap.start()

    def fine_valid(i):
        place = me * n + i - DEPTH
        return jnp.where((place >= 0) & (place < count * n), 1.0, 0.0)

    def coarse_valid(i):
        place = me * nc + i - side
        return jnp.where((place >= 0) & (place < count * nc), 1.0, 0.0)

    make_coefs(coef, kx, rx, DEPTH + 1, DEPTH + n - 1, 1, fine_valid)

    first_k.arrived()
    first_r.arrived()

    def unpack_k(which, low, rate_low):
        for i in range(DEPTH):
            kx[low + i] = load_plane(raw_k, which, i)
        for i in range(rate_rows):
            rx[rate_low + i] = load_plane(raw_r, which, i)

    when_left(lambda: unpack_k(0, 0, DEPTH - rate_rows))
    when_right(lambda: unpack_k(1, n + DEPTH, n + DEPTH))
    first_face(coef, kx, 0, fine_valid)
    make_coefs(coef, kx, rx, 1, DEPTH + 1, 1, fine_valid)
    make_coefs(coef, kx, rx, DEPTH + n - 1, ext - 1, 1, fine_valid)

    def fine_round(r, w):
        source = u.at[r, w]
        for k in range(1, DEPTH + 1):
            target = u.at[r + 1, w] if k == DEPTH else temp.at[k % 2]
            grid_step(source, target, coef, k, ext - k, 1)
            source = target

    def unpack_u(w, which, low):
        for i in range(DEPTH):
            u[0, w, low + i] = load_plane(raw_u, w, which, i)

    for w in range(windows):
        first_u[w].arrived()
        when_left(functools.partial(unpack_u, w, 0, 0))
        when_right(functools.partial(unpack_u, w, 1, n + DEPTH))
        fine_round(0, w)
        if ROUNDS > 1:
            round_swap(1, w).start()

    def coarse_run(source, target):
        for k in range(1, COARSE):
            dest = ctemp.at[k % 2]
            grid_step(source, dest, ccoef, k, cext - k, 2)
            source = dest
        grid_step(source, target, ccoef, COARSE, cext - COARSE, 2)

    coarse_k.arrived()
    coarse_r.arrived()
    first_face(ccoef, kc, 0, coarse_valid)
    make_coefs(ccoef, kc, rc, 1, cext - 1, 2, coarse_valid)
    for w in range(windows):
        coarse_old[w].arrived()
        coarse_run(cstate.at[w], old.at[w])

    def middle(r, _):
        for w in range(windows):
            round_swap(r, w).arrived()
            fine_round(r, w)
            round_swap(r + 1, w).start()
        return 0

    lax.fori_loop(1, ROUNDS - 1, middle, 0)

    def deltas(w, i):
        base = DEPTH + 2 * i
        ends = restrict_rows(u[ROUNDS, w, base], u[ROUNDS, w, base + 1])
        return (ends - old[w, side + i]) + newer[w, side + i]

    def carry_on(w):
        for i in range(nc):
            chain[w + 1, side + i] = deltas(w, i)

    def take_old():
        newer[0, pl.ds(side, nc)] = old[0, pl.ds(side, nc)]

    incoming = pltpu.make_async_remote_copy(
        src_ref=outgoing, dst_ref=passed, send_sem=tm_send, recv_sem=tm_recv,
        device_id={"tm": lax.rem(group + 1, groups)}, device_id_type=MESH,
    ) if groups > 1 else None

    for w in range(windows):
        if ROUNDS > 1:
            round_swap(ROUNDS - 1, w).arrived()
            fine_round(ROUNDS - 1, w)
        if w == 0:
            pl.when(group == 0)(take_old)
            if windows > 1:
                def start_chain():
                    carry_on(0)
                    coarse_chain[1].start()

                pl.when(group == 0)(start_chain)

    if groups > 1:
        def from_before():
            incoming.wait_recv()
            chain[0, pl.ds(side, nc)] = passed[...]
            coarse_chain[0].start()
            coarse_chain[0].arrived()
            coarse_run(chain.at[0], newer.at[0])
            if windows > 1:
                carry_on(0)
                coarse_chain[1].start()

        pl.when(group > 0)(from_before)

    for w in range(1, windows):
        coarse_chain[w].arrived()
        coarse_run(chain.at[w], newer.at[w])
        if w + 1 < windows:
            carry_on(w)
            coarse_chain[w + 1].start()

    if groups > 1:
        def to_next():
            for i in range(nc):
                outgoing[i] = deltas(windows - 1, i)
            incoming.start()

        pl.when(group < groups - 1)(to_next)

    def finish(i, _):
        for w in range(windows):
            change = prolong_rows(newer[w, side + i] - old[w, side + i])
            for half in range(2):
                plane = u[ROUNDS, w, DEPTH + 2 * i + half] + change
                for j in range(per):
                    out[w, 2 * i + half, pl.ds(j, 8, stride=per), :] = plane[8 * j : 8 * j + 8]
        return 0

    for i in range(nc):
        finish(i, 0)

    for swap in [first_k, first_r, coarse_k, coarse_r] + first_u + coarse_old + coarse_chain[1:]:
        swap.sent()

    def rounds_sent(r, _):
        for w in range(windows):
            round_swap(r, w).sent()
        return 0

    lax.fori_loop(1, ROUNDS, rounds_sent, 0)
    if groups > 1:
        pl.when(group > 0)(coarse_chain[0].sent)
        pl.when(group < groups - 1)(incoming.wait_send)


def shards(count, groups, states, kappa, rate):
    windows, n, rows, lanes = states.shape
    ext = n + 2 * DEPTH
    nc = n // 2
    cext = nc + 2 * COARSE
    crows = rows // 2
    slots = 3 * windows + 4 + ROUNDS * windows
    f32 = jnp.float32
    vmem = pl.BlockSpec(memory_space=pltpu.VMEM)
    return pl.pallas_call(
        functools.partial(kernel, count, groups),
        out_shape=jax.ShapeDtypeStruct(states.shape, f32),
        in_specs=[pl.BlockSpec(memory_space=pl.ANY)] * 3,
        out_specs=vmem,
        scratch_shapes=[
            pltpu.VMEM(states.shape, f32),
            pltpu.VMEM(kappa.shape, f32),
            pltpu.VMEM(rate.shape, f32),
            pltpu.VMEM((ROUNDS + 1, windows, ext, rows, lanes), f32),
            pltpu.VMEM((2, ext, rows, lanes), f32),
            pltpu.VMEM((windows, 2, DEPTH, rows, lanes), f32),
            pltpu.VMEM((2, DEPTH, rows, lanes), f32),
            pltpu.VMEM((2, max(DEPTH - 1, 1), rows, lanes), f32),
            pltpu.VMEM((ext, rows, lanes), f32),
            pltpu.VMEM((ext, rows, lanes), f32),
            pltpu.VMEM((5, ext, rows, lanes), f32),
            pltpu.VMEM((cext, crows, lanes), f32),
            pltpu.VMEM((cext, crows, lanes), f32),
            pltpu.VMEM((5, cext, crows, lanes), f32),
            pltpu.VMEM((2, cext, crows, lanes), f32),
            pltpu.VMEM((windows, cext, crows, lanes), f32),
            pltpu.VMEM((windows, cext, crows, lanes), f32),
            pltpu.VMEM((windows, cext, crows, lanes), f32),
            pltpu.VMEM((windows, cext, crows, lanes), f32),
            pltpu.VMEM((nc, crows, lanes), f32),
            pltpu.VMEM((nc, crows, lanes), f32),
            pltpu.SemaphoreType.DMA((slots, 2)),
            pltpu.SemaphoreType.DMA((slots, 2)),
            pltpu.SemaphoreType.DMA,
            pltpu.SemaphoreType.DMA,
            pltpu.SemaphoreType.DMA((3,)),
        ],
        compiler_params=pltpu.CompilerParams(
            collective_id=0, has_side_effects=True, vmem_limit_bytes=60 * 1024 * 1024
        ),
    )(states, kappa, rate)


def solution(mesh):
    in_specs = (P("tm", "space", None, None), P("space", None, None), P("space", None, None))
    out_specs = P("tm", "space", None, None)
    body = functools.partial(shards, mesh.shape["space"], mesh.shape["tm"])
    return jax.shard_map(body, mesh=mesh, in_specs=in_specs, out_specs=out_specs, check_vma=False)
```

```python
import functools

import jax
import jax.numpy as jnp
from jax import lax
from jax.experimental import pallas as pl
from jax.experimental.pallas import tpu as pltpu
from jax.sharding import PartitionSpec as P

STEPS = 12
COARSE = 3
DEPTH = 2
ROUNDS = STEPS // DEPTH
MESH = pl.DeviceIdType.MESH
A, R, XP, YP, ZP = range(5)


def y_next(plane):
    rows = plane.shape[0]
    return jnp.concatenate([plane[8:rows], pltpu.roll(plane[0:8], 7, 0)], axis=0)


def y_prev(plane):
    rows = plane.shape[0]
    return jnp.concatenate([pltpu.roll(plane[rows - 8 : rows], 1, 0), plane[0 : rows - 8]], axis=0)


def z_next(plane, stride):
    return pltpu.roll(plane, plane.shape[1] - stride, 1)


def z_prev(plane, stride):
    return pltpu.roll(plane, stride, 1)


def edge_masks(rows, lanes, stride):
    row = lax.broadcasted_iota(jnp.int32, (rows, lanes), 0)
    lane = lax.broadcasted_iota(jnp.int32, (rows, lanes), 1)
    return (
        jnp.where(row == rows - 1, 0.0, 1.0),
        jnp.where(row == 0, 0.0, 1.0),
        jnp.where(lane >= lanes - stride, 0.0, 1.0),
        jnp.where(lane < stride, 0.0, 1.0),
    )


def make_coefs(coef, field, reaction, low, high, stride, row_valid):
    rows, lanes = field.shape[-2:]
    y_up, y_down, z_up, z_down = edge_masks(rows, lanes, stride)
    for i in range(low, high):
        k = field[i]
        r = reaction[i]
        valid = row_valid(i)
        xp = 0.5 * (k + field[i + 1])
        xm = 0.5 * (k + field[i - 1])
        yp = 0.5 * (k + y_next(k) * y_up)
        ym = 0.5 * (k + y_prev(k) * y_down)
        zp = 0.5 * (k + z_next(k, stride) * z_up)
        zm = 0.5 * (k + z_prev(k, stride) * z_down)
        coef[A, i] = (1.0 + r - ((xp + xm) + (yp + ym) + (zp + zm))) * valid
        coef[R, i] = r * valid
        coef[XP, i] = xp * (valid * row_valid(i + 1))
        coef[YP, i] = yp * (y_up * valid)
        coef[ZP, i] = zp * (z_up * valid)


def first_face(coef, field, low, row_valid):
    both = row_valid(low) * row_valid(low + 1)
    coef[XP, low] = (0.5 * both) * (field[low] + field[low + 1])


def grid_step(source, target, coef, low, high, stride):
    before, u, before_face = source[low - 1], source[low], coef[XP, low - 1]
    for i in range(low, high):
        after = source[i + 1]
        face = coef[XP, i]
        y_face = coef[YP, i]
        z_face = coef[ZP, i]
        total = u * (coef[A, i] - coef[R, i] * (u * u))
        total = total + (face * after + before_face * before)
        total = total + (y_face * y_next(u) + y_prev(y_face * u))
        total = total + (z_face * z_next(u, stride) + z_prev(z_face * u, stride))
        target[i] = total
        before, u, before_face = u, after, face


def restrict_rows(first, second):
    both = first + second
    rows, lanes = both.shape
    pairs = jnp.concatenate(
        [both[j : j + 8] + both[j + 8 : j + 16] for j in range(0, rows, 16)], axis=0
    )
    lane = lax.broadcasted_iota(jnp.int32, pairs.shape, 1)
    other = jnp.where(lane % 2 == 0, z_next(pairs, 1), z_prev(pairs, 1))
    return (pairs + other) * 0.125


def even_lanes(plane):
    return lax.broadcasted_iota(jnp.int32, plane.shape, 1) % 2 == 0


def pack(first, second):
    return jnp.where(even_lanes(first), first, second)


def unpack(both):
    even = even_lanes(both)
    return jnp.where(even, both, z_prev(both, 1)), jnp.where(even, z_next(both, 1), both)


def prolong_rows(plane):
    rows = plane.shape[0]
    return jnp.concatenate(
        [plane[j : j + 8] for j in range(0, rows, 8) for _ in range(2)], axis=0
    )


def kernel(
    count, groups, states, kappa, rate, out,
    own_u, own_k, own_r, u, temp, raw_u, raw_k, raw_r, kx, rx, coef,
    kc, rc, kr, ccoef, ctemp, cstate, oldpair, old, chain, newer, passed, outgoing,
    send, recv, tm_send, tm_recv, local,
):
    windows, n, rows, lanes = states.shape
    ext = n + 2 * DEPTH
    nc = n // 2
    side = COARSE
    cext = nc + 2 * side
    per = rows // 8
    rate_rows = max(DEPTH - 1, 1)
    me = lax.axis_index("space")
    group = lax.axis_index("tm")
    left = lax.rem(me + count - 1, count)
    right = lax.rem(me + 1, count)
    has_left = me > 0
    has_right = me < count - 1

    def when_left(fn):
        pl.when(has_left)(fn)

    def when_right(fn):
        pl.when(has_right)(fn)

    class Swap:
        def __init__(self, head, tail, left_halo, right_halo, slot):
            self.to_left = pltpu.make_async_remote_copy(
                src_ref=head, dst_ref=right_halo, send_sem=send.at[slot, 0],
                recv_sem=recv.at[slot, 1], device_id={"space": left}, device_id_type=MESH,
            )
            self.to_right = pltpu.make_async_remote_copy(
                src_ref=tail, dst_ref=left_halo, send_sem=send.at[slot, 1],
                recv_sem=recv.at[slot, 0], device_id={"space": right}, device_id_type=MESH,
            )

        def start(self):
            when_left(self.to_left.start)
            when_right(self.to_right.start)

        def arrived(self):
            when_left(self.to_right.wait_recv)
            when_right(self.to_left.wait_recv)

        def sent(self):
            when_left(self.to_left.wait_send)
            when_right(self.to_right.wait_send)

    def padded_swap(ref, width, depth, slot):
        return Swap(
            ref.at[pl.ds(depth, depth)], ref.at[pl.ds(width, depth)],
            ref.at[pl.ds(0, depth)], ref.at[pl.ds(width + depth, depth)], slot,
        )

    pairs = (windows + 1) // 2
    slot_k, slot_r, slot_kr = (windows + i for i in range(3))
    slot_old = windows + 3
    slot_chain = slot_old + pairs
    slot_round = slot_chain + windows

    def raw_swap(source, target, depth, slot):
        return Swap(
            source.at[pl.ds(0, depth)], source.at[pl.ds(n - depth, depth)],
            target.at[0], target.at[1], slot,
        )

    first_u = [raw_swap(states.at[w], raw_u.at[w], DEPTH, w) for w in range(windows)]
    first_k = raw_swap(kappa, raw_k, DEPTH, slot_k)
    first_r = raw_swap(rate, raw_r, rate_rows, slot_r)
    coarse_kr = padded_swap(kr, nc, side, slot_kr)
    coarse_old = [padded_swap(cstate.at[p], nc, side, slot_old + p) for p in range(pairs)]
    coarse_chain = [padded_swap(chain.at[w], nc, side, slot_chain + w) for w in range(windows)]

    def round_swap(r, w):
        return padded_swap(u.at[r, w], n, DEPTH, slot_round + r * windows + w)

    loads = [
        pltpu.make_async_copy(source, target, local.at[i])
        for i, (source, target) in enumerate(((kappa, own_k), (rate, own_r), (states, own_u)))
    ]
    for load in loads:
        load.start()
    barrier = pltpu.get_barrier_semaphore()

    def greet(where):
        pl.semaphore_signal(barrier, inc=1, device_id=where, device_id_type=MESH)

    when_left(lambda: greet({"space": left}))
    when_right(lambda: greet({"space": right}))
    pl.when(group > 0)(lambda: greet({"tm": lax.rem(group + groups - 1, groups)}))
    pl.when(group < groups - 1)(lambda: greet({"tm": lax.rem(group + 1, groups)}))

    def load_plane(ref, *index):
        return jnp.concatenate(
            [ref[(*index, pl.ds(j, 8, stride=per), slice(None))] for j in range(per)], axis=0
        )

    def zero(ref, low, size):
        ref[pl.ds(low, size)] = jnp.zeros((size,) + ref.shape[1:], jnp.float32)

    def zero_side(fine_low, coarse_low):
        zero(kx, fine_low, DEPTH)
        zero(rx, fine_low, DEPTH)
        zero(kr, coarse_low, side)
        for p in range(pairs):
            zero(cstate.at[p], coarse_low, side)
        for w in range(windows):
            zero(chain.at[w], coarse_low, side)
            for r in range(ROUNDS):
                zero(u.at[r, w], fine_low, DEPTH)

    pl.when(me == 0)(lambda: zero_side(0, 0))
    pl.when(me == count - 1)(lambda: zero_side(n + DEPTH, nc + side))

    peers = [has_left, has_right, group > 0, group < groups - 1]
    pl.semaphore_wait(barrier, sum(jnp.where(there, 1, 0) for there in peers))

    first_k.start()
    first_r.start()
    for swap in first_u:
        swap.start()

    loads[0].wait()
    for i in range(n):
        kx[DEPTH + i] = load_plane(own_k, i)
    loads[1].wait()
    for i in range(n):
        rx[DEPTH + i] = load_plane(own_r, i)
    loads[2].wait()
    for w in range(windows):
        for i in range(n):
            u[0, w, DEPTH + i] = load_plane(own_u, w, i)

    for i in range(nc):
        base = DEPTH + 2 * i
        kc[side + i] = restrict_rows(kx[base], kx[base + 1])
        rc[side + i] = 4.0 * restrict_rows(rx[base], rx[base + 1])
        kr[side + i] = pack(kc[side + i], rc[side + i])
        for p in range(pairs):
            first, second = 2 * p, min(2 * p + 1, windows - 1)
            cstate[p, side + i] = pack(
                restrict_rows(u[0, first, base], u[0, first, base + 1]),
                restrict_rows(u[0, second, base], u[0, second, base + 1]),
            )
    coarse_kr.start()
    for swap in coarse_old:
        swap.start()

    def fine_valid(i):
        place = me * n + i - DEPTH
        return jnp.where((place >= 0) & (place < count * n), 1.0, 0.0)

    def coarse_valid(i):
        place = me * nc + i - side
        return jnp.where((place >= 0) & (place < count * nc), 1.0, 0.0)

    def fine_rows(r, w, spans):
        source = u.at[r, w]
        for k in range(1, DEPTH + 1):
            target = u.at[r + 1, w] if k == DEPTH else temp.at[w, k % 2]
            for low, high in spans(k):
                if low < high:
                    grid_step(source, target, coef, low, high, 1)
            source = target

    def inner(r, w):
        fine_rows(r, w, lambda k: [(DEPTH + k, n + DEPTH - k)])

    def outer(r, w):
        fine_rows(r, w, lambda k: [(k, DEPTH + k), (n + DEPTH - k, ext - k)])

    first_face(coef, kx, DEPTH, fine_valid)
    make_coefs(coef, kx, rx, DEPTH + 1, DEPTH + n - 1, 1, fine_valid)
    for w in range(windows):
        inner(0, w)

    first_k.arrived()
    first_r.arrived()

    def unpack_k(which, low, rate_low):
        for i in range(DEPTH):
            kx[low + i] = load_plane(raw_k, which, i)
        for i in range(rate_rows):
            rx[rate_low + i] = load_plane(raw_r, which, i)

    when_left(lambda: unpack_k(0, 0, DEPTH - rate_rows))
    when_right(lambda: unpack_k(1, n + DEPTH, n + DEPTH))
    first_face(coef, kx, 0, fine_valid)
    make_coefs(coef, kx, rx, 1, DEPTH + 1, 1, fine_valid)
    make_coefs(coef, kx, rx, DEPTH + n - 1, ext - 1, 1, fine_valid)

    def unpack_u(w, which, low):
        for i in range(DEPTH):
            u[0, w, low + i] = load_plane(raw_u, w, which, i)

    for w in range(windows):
        first_u[w].arrived()
        when_left(functools.partial(unpack_u, w, 0, 0))
        when_right(functools.partial(unpack_u, w, 1, n + DEPTH))
        outer(0, w)
        if ROUNDS > 1:
            round_swap(1, w).start()

    def coarse_run(source, target):
        for k in range(1, COARSE):
            dest = ctemp.at[k % 2]
            grid_step(source, dest, ccoef, k, cext - k, 2)
            source = dest
        grid_step(source, target, ccoef, COARSE, cext - COARSE, 2)

    coarse_kr.arrived()
    for i in list(range(side)) + list(range(nc + side, cext)):
        kc[i], rc[i] = unpack(kr[i])
    first_face(ccoef, kc, 0, coarse_valid)
    make_coefs(ccoef, kc, rc, 1, cext - 1, 2, coarse_valid)
    for p in range(pairs):
        coarse_old[p].arrived()
        coarse_run(cstate.at[p], oldpair.at[p])
        for i in range(side, side + nc):
            first, second = unpack(oldpair[p, i])
            old[2 * p, i] = first
            if 2 * p + 1 < windows:
                old[2 * p + 1, i] = second

    def middle(r, _):
        for w in range(windows):
            inner(r, w)
        for w in range(windows):
            round_swap(r, w).arrived()
            outer(r, w)
            round_swap(r + 1, w).start()
        return 0

    lax.fori_loop(1, ROUNDS - 1, middle, 0)

    def deltas(w, i):
        base = DEPTH + 2 * i
        ends = restrict_rows(u[ROUNDS, w, base], u[ROUNDS, w, base + 1])
        return (ends - old[w, side + i]) + newer[w, side + i]

    def carry_on(w):
        for i in range(nc):
            chain[w + 1, side + i] = deltas(w, i)

    def take_old():
        newer[0, pl.ds(side, nc)] = old[0, pl.ds(side, nc)]

    incoming = pltpu.make_async_remote_copy(
        src_ref=outgoing, dst_ref=passed, send_sem=tm_send, recv_sem=tm_recv,
        device_id={"tm": lax.rem(group + 1, groups)}, device_id_type=MESH,
    ) if groups > 1 else None

    for w in range(windows):
        if ROUNDS > 1:
            inner(ROUNDS - 1, w)
    for w in range(windows):
        if ROUNDS > 1:
            round_swap(ROUNDS - 1, w).arrived()
            outer(ROUNDS - 1, w)
        if w == 0:
            pl.when(group == 0)(take_old)
            if windows > 1:
                def start_chain():
                    carry_on(0)
                    coarse_chain[1].start()

                pl.when(group == 0)(start_chain)

    if groups > 1:
        def from_before():
            incoming.wait_recv()
            for i in range(nc // 2):
                chain[0, side + 2 * i], chain[0, side + 2 * i + 1] = unpack(passed[i])
            coarse_chain[0].start()
            coarse_chain[0].arrived()
            coarse_run(chain.at[0], newer.at[0])
            if windows > 1:
                carry_on(0)
                coarse_chain[1].start()

        pl.when(group > 0)(from_before)

    def finish(w):
        for i in range(nc):
            change = prolong_rows(newer[w, side + i] - old[w, side + i])
            for half in range(2):
                plane = u[ROUNDS, w, DEPTH + 2 * i + half] + change
                for j in range(per):
                    out[w, 2 * i + half, pl.ds(j, 8, stride=per), :] = plane[8 * j : 8 * j + 8]

    for w in range(1, windows):
        finish(w - 1)
        coarse_chain[w].arrived()
        coarse_run(chain.at[w], newer.at[w])
        if w + 1 < windows:
            carry_on(w)
            coarse_chain[w + 1].start()

    if groups > 1:
        def to_next():
            for i in range(nc // 2):
                outgoing[i] = pack(deltas(windows - 1, 2 * i), deltas(windows - 1, 2 * i + 1))
            incoming.start()

        pl.when(group < groups - 1)(to_next)

    finish(windows - 1)

    for swap in [first_k, first_r, coarse_kr] + first_u + coarse_old + coarse_chain[1:]:
        swap.sent()

    def rounds_sent(r, _):
        for w in range(windows):
            round_swap(r, w).sent()
        return 0

    lax.fori_loop(1, ROUNDS, rounds_sent, 0)
    if groups > 1:
        pl.when(group > 0)(coarse_chain[0].sent)
        pl.when(group < groups - 1)(incoming.wait_send)


def shards(count, groups, states, kappa, rate):
    windows, n, rows, lanes = states.shape
    ext = n + 2 * DEPTH
    nc = n // 2
    cext = nc + 2 * COARSE
    crows = rows // 2
    pairs = (windows + 1) // 2
    slots = 2 * windows + pairs + 3 + ROUNDS * windows
    f32 = jnp.float32
    vmem = pl.BlockSpec(memory_space=pltpu.VMEM)
    return pl.pallas_call(
        functools.partial(kernel, count, groups),
        out_shape=jax.ShapeDtypeStruct(states.shape, f32),
        in_specs=[pl.BlockSpec(memory_space=pl.ANY)] * 3,
        out_specs=vmem,
        scratch_shapes=[
            pltpu.VMEM(states.shape, f32),
            pltpu.VMEM(kappa.shape, f32),
            pltpu.VMEM(rate.shape, f32),
            pltpu.VMEM((ROUNDS + 1, windows, ext, rows, lanes), f32),
            pltpu.VMEM((windows, 2, ext, rows, lanes), f32),
            pltpu.VMEM((windows, 2, DEPTH, rows, lanes), f32),
            pltpu.VMEM((2, DEPTH, rows, lanes), f32),
            pltpu.VMEM((2, max(DEPTH - 1, 1), rows, lanes), f32),
            pltpu.VMEM((ext, rows, lanes), f32),
            pltpu.VMEM((ext, rows, lanes), f32),
            pltpu.VMEM((5, ext, rows, lanes), f32),
            pltpu.VMEM((cext, crows, lanes), f32),
            pltpu.VMEM((cext, crows, lanes), f32),
            pltpu.VMEM((cext, crows, lanes), f32),
            pltpu.VMEM((5, cext, crows, lanes), f32),
            pltpu.VMEM((2, cext, crows, lanes), f32),
            pltpu.VMEM((pairs, cext, crows, lanes), f32),
            pltpu.VMEM((pairs, cext, crows, lanes), f32),
            pltpu.VMEM((windows, cext, crows, lanes), f32),
            pltpu.VMEM((windows, cext, crows, lanes), f32),
            pltpu.VMEM((windows, cext, crows, lanes), f32),
            pltpu.VMEM((nc // 2, crows, lanes), f32),
            pltpu.VMEM((nc // 2, crows, lanes), f32),
            pltpu.SemaphoreType.DMA((slots, 2)),
            pltpu.SemaphoreType.DMA((slots, 2)),
            pltpu.SemaphoreType.DMA,
            pltpu.SemaphoreType.DMA,
            pltpu.SemaphoreType.DMA((3,)),
        ],
        compiler_params=pltpu.CompilerParams(
            collective_id=0, has_side_effects=True, vmem_limit_bytes=60 * 1024 * 1024
        ),
    )(states, kappa, rate)


def solution(mesh):
    in_specs = (P("tm", "space", None, None), P("space", None, None), P("space", None, None))
    out_specs = P("tm", "space", None, None)
    body = functools.partial(shards, mesh.shape["space"], mesh.shape["tm"])
    return jax.shard_map(body, mesh=mesh, in_specs=in_specs, out_specs=out_specs, check_vma=False)
```

```python
import functools

import jax
import jax.numpy as jnp
from jax import lax
from jax.experimental import pallas as pl
from jax.experimental.pallas import tpu as pltpu
from jax.sharding import PartitionSpec as P

STEPS = 12
COARSE = 3
DEPTH = 3
ROUNDS = STEPS // DEPTH
MESH = pl.DeviceIdType.MESH
A, R, XP, YP, ZP = range(5)


def y_next(plane):
    rows = plane.shape[0]
    return jnp.concatenate([plane[8:rows], pltpu.roll(plane[0:8], 7, 0)], axis=0)


def y_prev(plane):
    rows = plane.shape[0]
    return jnp.concatenate([pltpu.roll(plane[rows - 8 : rows], 1, 0), plane[0 : rows - 8]], axis=0)


def z_next(plane, stride):
    return pltpu.roll(plane, plane.shape[1] - stride, 1)


def z_prev(plane, stride):
    return pltpu.roll(plane, stride, 1)


def edge_masks(rows, lanes, stride):
    row = lax.broadcasted_iota(jnp.int32, (rows, lanes), 0)
    lane = lax.broadcasted_iota(jnp.int32, (rows, lanes), 1)
    return (
        jnp.where(row == rows - 1, 0.0, 1.0),
        jnp.where(row == 0, 0.0, 1.0),
        jnp.where(lane >= lanes - stride, 0.0, 1.0),
        jnp.where(lane < stride, 0.0, 1.0),
    )


def make_coefs(coef, field, reaction, low, high, stride, row_valid):
    rows, lanes = field.shape[-2:]
    y_up, y_down, z_up, z_down = edge_masks(rows, lanes, stride)
    for i in range(low, high):
        k = field[i]
        r = reaction[i]
        valid = row_valid(i)
        xp = 0.5 * (k + field[i + 1])
        xm = 0.5 * (k + field[i - 1])
        yp = 0.5 * (k + y_next(k) * y_up)
        ym = 0.5 * (k + y_prev(k) * y_down)
        zp = 0.5 * (k + z_next(k, stride) * z_up)
        zm = 0.5 * (k + z_prev(k, stride) * z_down)
        coef[A, i] = (1.0 + r - ((xp + xm) + (yp + ym) + (zp + zm))) * valid
        coef[R, i] = r * valid
        coef[XP, i] = xp * (valid * row_valid(i + 1))
        coef[YP, i] = yp * (y_up * valid)
        coef[ZP, i] = zp * (z_up * valid)


def first_face(coef, field, low, row_valid):
    both = row_valid(low) * row_valid(low + 1)
    coef[XP, low] = (0.5 * both) * (field[low] + field[low + 1])


def grid_step(source, target, coef, low, high, stride):
    before, u, before_face = source[low - 1], source[low], coef[XP, low - 1]
    for i in range(low, high):
        after = source[i + 1]
        face = coef[XP, i]
        y_face = coef[YP, i]
        z_face = coef[ZP, i]
        total = u * (coef[A, i] - coef[R, i] * (u * u))
        total = total + (face * after + before_face * before)
        total = total + (y_face * y_next(u) + y_prev(y_face * u))
        total = total + (z_face * z_next(u, stride) + z_prev(z_face * u, stride))
        target[i] = total
        before, u, before_face = u, after, face


def restrict_rows(first, second):
    both = first + second
    rows, lanes = both.shape
    pairs = jnp.concatenate(
        [both[j : j + 8] + both[j + 8 : j + 16] for j in range(0, rows, 16)], axis=0
    )
    lane = lax.broadcasted_iota(jnp.int32, pairs.shape, 1)
    other = jnp.where(lane % 2 == 0, z_next(pairs, 1), z_prev(pairs, 1))
    return (pairs + other) * 0.125


def even_lanes(plane):
    return lax.broadcasted_iota(jnp.int32, plane.shape, 1) % 2 == 0


def pack(first, second):
    return jnp.where(even_lanes(first), first, second)


def unpack(both):
    even = even_lanes(both)
    return jnp.where(even, both, z_prev(both, 1)), jnp.where(even, z_next(both, 1), both)


def prolong_rows(plane):
    rows = plane.shape[0]
    return jnp.concatenate(
        [plane[j : j + 8] for j in range(0, rows, 8) for _ in range(2)], axis=0
    )


def kernel(
    count, groups, states, kappa, rate, out,
    own_u, own_k, own_r, u, temp, raw_u, raw_k, raw_r, kx, rx, coef,
    kc, rc, kr, ccoef, ctemp, cstate, oldpair, old, chain, newer, passed, outgoing,
    send, recv, tm_send, tm_recv, local,
):
    windows, n, rows, lanes = states.shape
    ext = n + 2 * DEPTH
    nc = n // 2
    side = COARSE
    cext = nc + 2 * side
    per = rows // 8
    rate_rows = max(DEPTH - 1, 1)
    me = lax.axis_index("space")
    group = lax.axis_index("tm")
    left = lax.rem(me + count - 1, count)
    right = lax.rem(me + 1, count)
    has_left = me > 0
    has_right = me < count - 1

    def when_left(fn):
        pl.when(has_left)(fn)

    def when_right(fn):
        pl.when(has_right)(fn)

    class Swap:
        def __init__(self, head, tail, left_halo, right_halo, slot):
            self.to_left = pltpu.make_async_remote_copy(
                src_ref=head, dst_ref=right_halo, send_sem=send.at[slot, 0],
                recv_sem=recv.at[slot, 1], device_id={"space": left}, device_id_type=MESH,
            )
            self.to_right = pltpu.make_async_remote_copy(
                src_ref=tail, dst_ref=left_halo, send_sem=send.at[slot, 1],
                recv_sem=recv.at[slot, 0], device_id={"space": right}, device_id_type=MESH,
            )

        def start(self):
            when_left(self.to_left.start)
            when_right(self.to_right.start)

        def arrived(self):
            when_left(self.to_right.wait_recv)
            when_right(self.to_left.wait_recv)

        def sent(self):
            when_left(self.to_left.wait_send)
            when_right(self.to_right.wait_send)

    def padded_swap(ref, width, depth, slot):
        return Swap(
            ref.at[pl.ds(depth, depth)], ref.at[pl.ds(width, depth)],
            ref.at[pl.ds(0, depth)], ref.at[pl.ds(width + depth, depth)], slot,
        )

    pairs = (windows + 1) // 2
    slot_k, slot_r, slot_kr = (windows + i for i in range(3))
    slot_old = windows + 3
    slot_chain = slot_old + pairs
    slot_round = slot_chain + windows

    def raw_swap(source, target, depth, slot):
        return Swap(
            source.at[pl.ds(0, depth)], source.at[pl.ds(n - depth, depth)],
            target.at[0], target.at[1], slot,
        )

    first_u = [raw_swap(states.at[w], raw_u.at[w], DEPTH, w) for w in range(windows)]
    first_k = raw_swap(kappa, raw_k, DEPTH, slot_k)
    first_r = raw_swap(rate, raw_r, rate_rows, slot_r)
    coarse_kr = padded_swap(kr, nc, side, slot_kr)
    coarse_old = [padded_swap(cstate.at[p], nc, side, slot_old + p) for p in range(pairs)]
    coarse_chain = [padded_swap(chain.at[w], nc, side, slot_chain + w) for w in range(windows)]

    def round_swap(r, w):
        return padded_swap(u.at[r, w], n, DEPTH, slot_round + r * windows + w)

    loads = [
        pltpu.make_async_copy(source, target, local.at[i])
        for i, (source, target) in enumerate(((kappa, own_k), (rate, own_r), (states, own_u)))
    ]
    for load in loads:
        load.start()
    barrier = pltpu.get_barrier_semaphore()

    def greet(where):
        pl.semaphore_signal(barrier, inc=1, device_id=where, device_id_type=MESH)

    when_left(lambda: greet({"space": left}))
    when_right(lambda: greet({"space": right}))
    pl.when(group > 0)(lambda: greet({"tm": lax.rem(group + groups - 1, groups)}))
    pl.when(group < groups - 1)(lambda: greet({"tm": lax.rem(group + 1, groups)}))

    def load_plane(ref, *index):
        return jnp.concatenate(
            [ref[(*index, pl.ds(j, 8, stride=per), slice(None))] for j in range(per)], axis=0
        )

    def zero(ref, low, size):
        ref[pl.ds(low, size)] = jnp.zeros((size,) + ref.shape[1:], jnp.float32)

    def zero_side(fine_low, coarse_low):
        zero(kx, fine_low, DEPTH)
        zero(rx, fine_low, DEPTH)
        zero(kr, coarse_low, side)
        for p in range(pairs):
            zero(cstate.at[p], coarse_low, side)
        for w in range(windows):
            zero(chain.at[w], coarse_low, side)
            for r in range(ROUNDS):
                zero(u.at[r, w], fine_low, DEPTH)

    pl.when(me == 0)(lambda: zero_side(0, 0))
    pl.when(me == count - 1)(lambda: zero_side(n + DEPTH, nc + side))

    peers = [has_left, has_right, group > 0, group < groups - 1]
    pl.semaphore_wait(barrier, sum(jnp.where(there, 1, 0) for there in peers))

    first_k.start()
    first_r.start()
    for swap in first_u:
        swap.start()

    loads[0].wait()
    for i in range(n):
        kx[DEPTH + i] = load_plane(own_k, i)
    loads[1].wait()
    for i in range(n):
        rx[DEPTH + i] = load_plane(own_r, i)
    loads[2].wait()
    for w in range(windows):
        for i in range(n):
            u[0, w, DEPTH + i] = load_plane(own_u, w, i)

    for i in range(nc):
        base = DEPTH + 2 * i
        kc[side + i] = restrict_rows(kx[base], kx[base + 1])
        rc[side + i] = 4.0 * restrict_rows(rx[base], rx[base + 1])
        kr[side + i] = pack(kc[side + i], rc[side + i])
        for p in range(pairs):
            first, second = 2 * p, min(2 * p + 1, windows - 1)
            cstate[p, side + i] = pack(
                restrict_rows(u[0, first, base], u[0, first, base + 1]),
                restrict_rows(u[0, second, base], u[0, second, base + 1]),
            )
    coarse_kr.start()
    for swap in coarse_old:
        swap.start()

    def fine_valid(i):
        place = me * n + i - DEPTH
        return jnp.where((place >= 0) & (place < count * n), 1.0, 0.0)

    def coarse_valid(i):
        place = me * nc + i - side
        return jnp.where((place >= 0) & (place < count * nc), 1.0, 0.0)

    def fine_rows(r, w, spans):
        source = u.at[r, w]
        for k in range(1, DEPTH + 1):
            target = u.at[r + 1, w] if k == DEPTH else temp.at[w, k % 2]
            for low, high in spans(k):
                if low < high:
                    grid_step(source, target, coef, low, high, 1)
            source = target

    def inner(r, w):
        fine_rows(r, w, lambda k: [(DEPTH + k, n + DEPTH - k)])

    def outer(r, w):
        fine_rows(r, w, lambda k: [(k, DEPTH + k), (n + DEPTH - k, ext - k)])

    first_face(coef, kx, DEPTH, fine_valid)
    make_coefs(coef, kx, rx, DEPTH + 1, DEPTH + n - 1, 1, fine_valid)
    for w in range(windows):
        inner(0, w)

    first_k.arrived()
    first_r.arrived()

    def unpack_k(which, low, rate_low):
        for i in range(DEPTH):
            kx[low + i] = load_plane(raw_k, which, i)
        for i in range(rate_rows):
            rx[rate_low + i] = load_plane(raw_r, which, i)

    when_left(lambda: unpack_k(0, 0, DEPTH - rate_rows))
    when_right(lambda: unpack_k(1, n + DEPTH, n + DEPTH))
    first_face(coef, kx, 0, fine_valid)
    make_coefs(coef, kx, rx, 1, DEPTH + 1, 1, fine_valid)
    make_coefs(coef, kx, rx, DEPTH + n - 1, ext - 1, 1, fine_valid)

    def unpack_u(w, which, low):
        for i in range(DEPTH):
            u[0, w, low + i] = load_plane(raw_u, w, which, i)

    for w in range(windows):
        first_u[w].arrived()
        when_left(functools.partial(unpack_u, w, 0, 0))
        when_right(functools.partial(unpack_u, w, 1, n + DEPTH))
        outer(0, w)
        if ROUNDS > 1:
            round_swap(1, w).start()

    def coarse_run(source, target):
        for k in range(1, COARSE):
            dest = ctemp.at[k % 2]
            grid_step(source, dest, ccoef, k, cext - k, 2)
            source = dest
        grid_step(source, target, ccoef, COARSE, cext - COARSE, 2)

    coarse_kr.arrived()
    for i in list(range(side)) + list(range(nc + side, cext)):
        kc[i], rc[i] = unpack(kr[i])
    first_face(ccoef, kc, 0, coarse_valid)
    make_coefs(ccoef, kc, rc, 1, cext - 1, 2, coarse_valid)
    for p in range(pairs):
        coarse_old[p].arrived()
        coarse_run(cstate.at[p], oldpair.at[p])
        for i in range(side, side + nc):
            first, second = unpack(oldpair[p, i])
            old[2 * p, i] = first
            if 2 * p + 1 < windows:
                old[2 * p + 1, i] = second

    def middle(r, _):
        for w in range(windows):
            inner(r, w)
        for w in range(windows):
            round_swap(r, w).arrived()
            outer(r, w)
            round_swap(r + 1, w).start()
        return 0

    lax.fori_loop(1, ROUNDS - 1, middle, 0)

    def deltas(w, i):
        base = DEPTH + 2 * i
        ends = restrict_rows(u[ROUNDS, w, base], u[ROUNDS, w, base + 1])
        return (ends - old[w, side + i]) + newer[w, side + i]

    def carry_on(w):
        for i in range(nc):
            chain[w + 1, side + i] = deltas(w, i)

    def take_old():
        newer[0, pl.ds(side, nc)] = old[0, pl.ds(side, nc)]

    incoming = pltpu.make_async_remote_copy(
        src_ref=outgoing, dst_ref=passed, send_sem=tm_send, recv_sem=tm_recv,
        device_id={"tm": lax.rem(group + 1, groups)}, device_id_type=MESH,
    ) if groups > 1 else None

    for w in range(windows):
        if ROUNDS > 1:
            inner(ROUNDS - 1, w)
    for w in range(windows):
        if ROUNDS > 1:
            round_swap(ROUNDS - 1, w).arrived()
            outer(ROUNDS - 1, w)
        if w == 0:
            pl.when(group == 0)(take_old)
            if windows > 1:
                def start_chain():
                    carry_on(0)
                    coarse_chain[1].start()

                pl.when(group == 0)(start_chain)

    if groups > 1:
        def from_before():
            incoming.wait_recv()
            for i in range(nc // 2):
                chain[0, side + 2 * i], chain[0, side + 2 * i + 1] = unpack(passed[i])
            coarse_chain[0].start()
            coarse_chain[0].arrived()
            coarse_run(chain.at[0], newer.at[0])
            if windows > 1:
                carry_on(0)
                coarse_chain[1].start()

        pl.when(group > 0)(from_before)

    def finish(w):
        for i in range(nc):
            change = prolong_rows(newer[w, side + i] - old[w, side + i])
            for half in range(2):
                plane = u[ROUNDS, w, DEPTH + 2 * i + half] + change
                for j in range(per):
                    out[w, 2 * i + half, pl.ds(j, 8, stride=per), :] = plane[8 * j : 8 * j + 8]

    for w in range(1, windows):
        finish(w - 1)
        coarse_chain[w].arrived()
        coarse_run(chain.at[w], newer.at[w])
        if w + 1 < windows:
            carry_on(w)
            coarse_chain[w + 1].start()

    if groups > 1:
        def to_next():
            for i in range(nc // 2):
                outgoing[i] = pack(deltas(windows - 1, 2 * i), deltas(windows - 1, 2 * i + 1))
            incoming.start()

        pl.when(group < groups - 1)(to_next)

    finish(windows - 1)

    for swap in [first_k, first_r, coarse_kr] + first_u + coarse_old + coarse_chain[1:]:
        swap.sent()

    def rounds_sent(r, _):
        for w in range(windows):
            round_swap(r, w).sent()
        return 0

    lax.fori_loop(1, ROUNDS, rounds_sent, 0)
    if groups > 1:
        pl.when(group > 0)(coarse_chain[0].sent)
        pl.when(group < groups - 1)(incoming.wait_send)


def shards(count, groups, states, kappa, rate):
    windows, n, rows, lanes = states.shape
    ext = n + 2 * DEPTH
    nc = n // 2
    cext = nc + 2 * COARSE
    crows = rows // 2
    pairs = (windows + 1) // 2
    slots = 2 * windows + pairs + 3 + ROUNDS * windows
    f32 = jnp.float32
    vmem = pl.BlockSpec(memory_space=pltpu.VMEM)
    return pl.pallas_call(
        functools.partial(kernel, count, groups),
        out_shape=jax.ShapeDtypeStruct(states.shape, f32),
        in_specs=[pl.BlockSpec(memory_space=pl.ANY)] * 3,
        out_specs=vmem,
        scratch_shapes=[
            pltpu.VMEM(states.shape, f32),
            pltpu.VMEM(kappa.shape, f32),
            pltpu.VMEM(rate.shape, f32),
            pltpu.VMEM((ROUNDS + 1, windows, ext, rows, lanes), f32),
            pltpu.VMEM((windows, 2, ext, rows, lanes), f32),
            pltpu.VMEM((windows, 2, DEPTH, rows, lanes), f32),
            pltpu.VMEM((2, DEPTH, rows, lanes), f32),
            pltpu.VMEM((2, max(DEPTH - 1, 1), rows, lanes), f32),
            pltpu.VMEM((ext, rows, lanes), f32),
            pltpu.VMEM((ext, rows, lanes), f32),
            pltpu.VMEM((5, ext, rows, lanes), f32),
            pltpu.VMEM((cext, crows, lanes), f32),
            pltpu.VMEM((cext, crows, lanes), f32),
            pltpu.VMEM((cext, crows, lanes), f32),
            pltpu.VMEM((5, cext, crows, lanes), f32),
            pltpu.VMEM((2, cext, crows, lanes), f32),
            pltpu.VMEM((pairs, cext, crows, lanes), f32),
            pltpu.VMEM((pairs, cext, crows, lanes), f32),
            pltpu.VMEM((windows, cext, crows, lanes), f32),
            pltpu.VMEM((windows, cext, crows, lanes), f32),
            pltpu.VMEM((windows, cext, crows, lanes), f32),
            pltpu.VMEM((nc // 2, crows, lanes), f32),
            pltpu.VMEM((nc // 2, crows, lanes), f32),
            pltpu.SemaphoreType.DMA((slots, 2)),
            pltpu.SemaphoreType.DMA((slots, 2)),
            pltpu.SemaphoreType.DMA,
            pltpu.SemaphoreType.DMA,
            pltpu.SemaphoreType.DMA((3,)),
        ],
        compiler_params=pltpu.CompilerParams(
            collective_id=0, has_side_effects=True, vmem_limit_bytes=60 * 1024 * 1024
        ),
    )(states, kappa, rate)


def solution(mesh):
    in_specs = (P("tm", "space", None, None), P("space", None, None), P("space", None, None))
    out_specs = P("tm", "space", None, None)
    body = functools.partial(shards, mesh.shape["space"], mesh.shape["tm"])
    return jax.shard_map(body, mesh=mesh, in_specs=in_specs, out_specs=out_specs, check_vma=False)
```
